256 devices in a mesh: seq: 16 (over y, z_hi), pool: 2 (over z_lo), dp: 8 (over x, core).
Axes of the slice: x: 4, y: 4, z: 8 (z_hi: 4, z_lo: 2; z = z_hi * 2 + z_lo), core: 2. Of those that a mesh axis runs over, the one named last changes fastest.
Arguments:
- queries: bfloat16 [8, 2, 2048, 4096], P('dp', 'pool', 'seq'), may hold values from -160 to 160
- keys: bfloat16 [8, 2, 2048, 512], P('dp', 'pool', 'seq'), may hold values from -5 to 5
- values: bfloat16 [8, 2, 2048, 512], P('dp', 'pool', 'seq'), may hold values from -6 to 6
- old_keys: bfloat16 [8, 2, 512, 512], P('dp', 'pool', 'seq'), may hold values from -6 to 6
- old_values: bfloat16 [8, 2, 512, 512], P('dp', 'pool', 'seq'), may hold values from -6 to 6
- out_grad: bfloat16 [8, 2, 2048, 4096], P('dp', 'pool', 'seq'), may hold values from -6 to 6
- inputs: bfloat16 [8, 2, 2048, 8192], P('dp', 'pool', 'seq'), may hold values from -6 to 6
- reads: int32 [8, 2, 2, 4], P('dp', 'pool'), may hold values 0 or 1
Outputs:
- query_grad: bfloat16 [8, 2, 2048, 4096], P('dp', 'pool', 'seq')
- key_grad: bfloat16 [8, 2, 2048, 512], P('dp', 'pool', 'seq')
- value_grad: bfloat16 [8, 2, 2048, 512], P('dp', 'pool', 'seq')
- old_key_grad: bfloat16 [8, 2, 512, 512], P('dp', 'pool', 'seq')
- old_value_grad: bfloat16 [8, 2, 512, 512], P('dp', 'pool', 'seq')
- weight_grad: bfloat16 [8192, 512], P(('seq', 'pool'))
The draws below stay inside these ranges and needn't reach their ends.
All inputs are finite; a program needn't handle non-finite values. No bound on the sum of `reads` on one device may be relied on, other than what follows from the above.
Results may differ from the reference program's by a relative error of at most 0.025.
Values may be sent and summed in bfloat16 or wider, within the bound.
A program may use at most 128 MiB of HBM per device.

```python
import jax
import jax.numpy as jnp
from jax import lax

D = 8192
HQ = 32
KVH = 4
HD = 128
QCHUNKS = 2
OLD_STRETCHES = 4
GROUP = 8
CUR = 2048
OLD = 512
BATCHES = 8
HOLDERS = 2
N_SEQ = 16
N_POOL = 2
N_DP = 8


def shared_keys(key):
    base = jnp.clip(jax.random.normal(key, (BATCHES, HOLDERS, CUR, KVH * HD), jnp.float32), -5.0, 5.0)
    return base


def draw_keys(key, part):
    return shared_keys(key).astype(jnp.bfloat16)


def draw_queries(key, part):
    key = jax.random.fold_in(key, 2)
    base = jnp.clip(jax.random.normal(key, (BATCHES, HOLDERS, CUR, HQ * HD), jnp.float32), -5.0, 5.0)
    return base.astype(jnp.bfloat16)


def place_ends(values, stream_key, low, top_value):
    place = [jax.random.randint(jax.random.fold_in(stream_key, axis), (), 0, length) for axis, length in enumerate(values.shape)]
    widest = values.shape.index(max(values.shape))
    neighbour = place[:widest] + [(place[widest] + 1) % values.shape[widest]] + place[widest + 1:]
    return values.at[tuple(place)].set(low).at[tuple(neighbour)].set(top_value)


def block_scale(stream_key, extent, shards, smallest, top_value):
    gain, own = 1.0, jax.random.fold_in(stream_key, 6)
    for dim, parts in shards:
        heights = jnp.exp(jax.random.uniform(jax.random.fold_in(own, dim), (parts,), jnp.float32, smallest / len(shards), top_value / len(shards)))
        gain = gain * jnp.repeat(heights, extent[dim] // parts).reshape([-1 if axis == dim else 1 for axis in range(len(extent))])
    return gain


def scatter_about(rng, shape, width, bound, shards=(), held_as=jnp.bfloat16):
    entries = jax.random.normal(rng, shape, jnp.float32) * width
    if len(shards) > 0:
        entries = block_scale(rng, shape, shards, -0.22, 0.18) * entries
    return jnp.clip(entries, min=-bound, max=bound).astype(held_as)


def setup_inputs(seed: int = 0) -> dict:
    arg_keys = jax.random.split(jax.random.key(seed), 9)
    return {
        "queries": draw_queries(jax.random.fold_in(arg_keys[8], 71), 0),
        "keys": draw_keys(jax.random.fold_in(arg_keys[8], 71), 0),
        "values": scatter_about(arg_keys[2], (BATCHES, HOLDERS, CUR, KVH * HD), 1.0, 6.0, ((0, 8), (1, 2), (2, 16))),
        "old_keys": scatter_about(arg_keys[3], (BATCHES, HOLDERS, OLD, KVH * HD), 1.0, 6.0, ((0, 8), (1, 2), (2, 16))),
        "old_values": scatter_about(arg_keys[4], (BATCHES, HOLDERS, OLD, KVH * HD), 1.0, 6.0, ((0, 8), (1, 2), (2, 16))),
        "out_grad": scatter_about(arg_keys[5], (BATCHES, HOLDERS, CUR, HQ * HD), 1.0, 6.0, ((0, 8), (1, 2), (2, 16))),
        "inputs": scatter_about(arg_keys[6], (BATCHES, HOLDERS, CUR, D), 1.0, 6.0, ((0, 8), (1, 2), (2, 16))),
        "reads": place_ends((jax.random.randint(arg_keys[7], (BATCHES, HOLDERS, QCHUNKS, OLD_STRETCHES), 0, 2) < 1).astype(jnp.int32), jax.random.fold_in(arg_keys[7], 1), 0, 1),
    }


NEG = -1e30


def allowed_keys(reads_seq):
    rows = jnp.arange(CUR)
    query_stretch = rows // (CUR // QCHUNKS)
    old_stretch = jnp.arange(OLD) // (OLD // OLD_STRETCHES)
    row_reads = reads_seq[query_stretch]
    old_ok = row_reads[:, old_stretch] > 0
    cur_ok = jnp.arange(CUR)[None, :] <= rows[:, None]
    return jnp.concatenate([old_ok, cur_ok], 1)


def one_sequence(items):
    queries_s, grad_s, keys_s, values_s, past_k, past_v, reads_s = items
    allowed = allowed_keys(reads_s)
    all_k = jnp.concatenate([past_k, keys_s], 0)
    all_v = jnp.concatenate([past_v, values_s], 0)
    total = OLD + CUR
    scale = HD ** -0.5
    heads_dev = HQ // N_SEQ
    sharers = GROUP // heads_dev

    def one_group(index):
        start = (index * GROUP * HD).astype(jnp.int32)
        q_group = lax.dynamic_slice_in_dim(queries_s, start, GROUP * HD, 1).reshape(CUR, GROUP, HD).astype(jnp.float32)
        g_group = lax.dynamic_slice_in_dim(grad_s, start, GROUP * HD, 1).reshape(CUR, GROUP, HD).astype(jnp.float32)
        col = (index * HD).astype(jnp.int32)
        k_group = lax.dynamic_slice_in_dim(all_k, col, HD, 1).astype(jnp.float32)
        v_group = lax.dynamic_slice_in_dim(all_v, col, HD, 1).astype(jnp.float32)
        scores = jnp.einsum("qhd,kd->hqk", q_group, k_group) * scale
        scores = jnp.where(allowed[None], scores, NEG)
        top = jnp.max(scores, -1, keepdims=True)
        expo = jnp.exp(scores - top)
        probs = expo / jnp.sum(expo, -1, keepdims=True)
        dprobs = jnp.einsum("qhd,kd->hqk", g_group, v_group)
        delta = jnp.sum(probs * dprobs, -1, keepdims=True)
        dscores = lax.optimization_barrier((probs * (dprobs - delta)).astype(jnp.bfloat16)).astype(jnp.float32)
        probs_low = lax.optimization_barrier(probs.astype(jnp.bfloat16)).astype(jnp.float32)
        grad_q = (jnp.einsum("hqk,kd->qhd", dscores, k_group) * scale).astype(jnp.bfloat16)
        grad_k = jnp.einsum("hqk,qhd->hkd", dscores, q_group) * scale
        grad_v = jnp.einsum("hqk,qhd->hkd", probs_low, g_group)
        part_k = jnp.sum(grad_k.reshape(sharers, heads_dev, total, HD), 1).astype(jnp.bfloat16)
        part_v = jnp.sum(grad_v.reshape(sharers, heads_dev, total, HD), 1).astype(jnp.bfloat16)
        part_k = lax.optimization_barrier(part_k).astype(jnp.float32)
        part_v = lax.optimization_barrier(part_v).astype(jnp.float32)
        return grad_q.reshape(CUR, GROUP * HD), jnp.sum(part_k, 0), jnp.sum(part_v, 0)

    grad_q, grad_k, grad_v = lax.map(one_group, jnp.arange(KVH))
    grad_q = grad_q.transpose(1, 0, 2).reshape(CUR, HQ * HD)
    grad_k = grad_k.transpose(1, 0, 2).reshape(total, KVH * HD).astype(jnp.bfloat16)
    grad_v = grad_v.transpose(1, 0, 2).reshape(total, KVH * HD).astype(jnp.bfloat16)
    return grad_q, grad_k[OLD:], grad_v[OLD:], grad_k[:OLD], grad_v[:OLD]


def flatten(array):
    return array.reshape((BATCHES * HOLDERS,) + array.shape[2:])


def reference(queries, keys, values, old_keys, old_values, out_grad, inputs, reads):
    items = (flatten(queries), flatten(out_grad), flatten(keys), flatten(values),
             flatten(jnp.flip(old_keys, 1)), flatten(jnp.flip(old_values, 1)), flatten(reads))
    grad_q, grad_k, grad_v, past_gk, past_gv = lax.map(one_sequence, items)
    shape_cur = (BATCHES, HOLDERS, CUR, KVH * HD)
    shape_old = (BATCHES, HOLDERS, OLD, KVH * HD)
    query_grad = grad_q.reshape(BATCHES, HOLDERS, CUR, HQ * HD)
    key_grad = grad_k.reshape(shape_cur)
    value_grad = grad_v.reshape(shape_cur)
    old_key_grad = jnp.flip(past_gk.reshape(shape_old), 1)
    old_value_grad = jnp.flip(past_gv.reshape(shape_old), 1)
    rows_all = inputs.reshape(BATCHES * HOLDERS * CUR, D)
    grads_all = value_grad.reshape(BATCHES * HOLDERS * CUR, KVH * HD)
    weight = lax.dot_general(rows_all, grads_all, (((0,), (0,)), ((), ())), preferred_element_type=jnp.float32)
    weight_grad = (weight / (N_SEQ * N_POOL * N_DP)).astype(jnp.bfloat16)
    return query_grad, key_grad, value_grad, old_key_grad, old_value_grad, weight_grad
```

```python
import jax
import jax.numpy as jnp
from jax import lax
from jax.experimental import pallas as pl
from jax.experimental.pallas import tpu as pltpu
from jax.sharding import PartitionSpec as P

MESH = pl.DeviceIdType.MESH
BF = jnp.bfloat16
F32 = jnp.float32
HD = 128
NY = 4
NJ = 4
NDP = 8
TOK = 128
OLDT = 32
ROWS = 1024
CHUNK = 512
SCALE = HD**-0.5
EXPC = SCALE * 1.4426950408889634
NEG = -1e30
UNITS = [(i, c) for i in range(4) for c in range(i + 2)]
UNIT = {u: n for n, u in enumerate(UNITS)}


def dot(a, b):
    return jnp.dot(a, b, preferred_element_type=F32)


def dot_nt(a, b):
    return lax.dot_general(a, b, (((1,), (1,)), ((), ())), preferred_element_type=F32)


def kernel(
    q_ref, k_ref, v_ref, ok_ref, ov_ref, g_ref, x_ref, bias_ref,
    dq_ref, dk_ref, dv_ref, odk_ref, odv_ref, dw_ref,
    xin, xloc, xall, qb, gb, kc, ko, kst, kt, ebuf, sbuf, linv, gl, ql, dqb,
    part, opart, oown, cown, m1, m2, m3, mrg, rold, vg4, og4, vgall,
    wp, wown, ry, wz, rz, wfin, ssem, rsem, lsem,
):
    seq = lax.axis_index("seq")
    p = lax.axis_index("pool")
    dp = lax.axis_index("dp")
    y = seq // NJ
    j = seq % NJ
    z = 2 * j + p
    x = dp // 2
    core = dp % 2
    jr = (j + 1) % NJ
    jl = (j + 3) % NJ
    jo = (j + 2) % NJ

    def at_y(yy):
        return (yy * NJ + j, p, dp)

    def at_j(jj, pp=None):
        return (y * NJ + jj, p if pp is None else pp, dp)

    def at_dp(dd):
        return (seq, p, dd)

    count = {"s": 0, "r": 0, "l": 0}
    sends = []

    def take(kind, n=1):
        base = count[kind]
        count[kind] += n
        return base

    def send(src, dst, rs, dev):
        c = pltpu.make_async_remote_copy(
            src_ref=src, dst_ref=dst, send_sem=ssem.at[take("s")], recv_sem=rsem.at[rs],
            device_id=dev, device_id_type=MESH,
        )
        c.start()
        sends.append(c)

    def arrived(dst, rs):
        pltpu.make_async_copy(dst, dst, rsem.at[rs]).wait()

    def local(src, dst):
        c = pltpu.make_async_copy(src, dst, lsem.at[take("l")])
        c.start()
        return c

    barrier = pltpu.get_barrier_semaphore()
    peers = [at_y((y + r) % NY) for r in range(1, NY)]
    peers += [at_j(((z + t) % 8) // 2, ((z + t) % 8) % 2) for t in range(1, 8)]
    peers += [at_dp((dp + t) % NDP) for t in range(1, NDP)]
    for dev in peers:
        pl.semaphore_signal(barrier, inc=1, device_id=dev, device_id_type=MESH)
    pl.semaphore_wait(barrier, len(peers))

    def col(n, width=HD):
        return pl.ds(pl.multiple_of(n * width, width), width)

    r_kv = [[take("r") for _ in range(3)] for _ in range(2)]
    r_ov = [[take("r") for _ in range(3)] for _ in range(2)]
    r_q = take("r", 4)
    r_g = take("r", 4)
    loc_x = local(x_ref, xin)
    loc_kv = []
    for a, (cur, old) in enumerate(((k_ref, ok_ref), (v_ref, ov_ref))):
        loc_kv.append((local(cur.at[:, col(y)], kc.at[a, y, j]), local(old.at[:, col(y)], kst.at[a, y])))
        for r in range(1, NY):
            yy = (y + r) % NY
            send(cur.at[:, col(yy)], kc.at[a, y, j], r_kv[a][r - 1], at_y(yy))
            send(old.at[:, col(yy)], kst.at[a, y], r_ov[a][r - 1], at_y(yy))
    loc_q = local(q_ref.at[:, col(y, ROWS)], qb.at[y])
    loc_g = local(g_ref.at[:, col(y, ROWS)], gb.at[y])
    for r in range(1, NY):
        yy = (y + r) % NY
        send(q_ref.at[:, col(yy, ROWS)], qb.at[y], r_q + r, at_y(yy))

    r_side = [[take("r"), take("r")] for _ in range(2)]
    r_fwd = [[take("r"), take("r")] for _ in range(2)]
    r_oz = [take("r", 4) for _ in range(2)]

    def gather_start(a):
        loc_kv[a][0].wait()
        loc_kv[a][1].wait()
        for r in range(1, NY):
            yy = (y + NY - r) % NY
            arrived(kc.at[a, yy, j], r_kv[a][r - 1])
            arrived(kst.at[a, yy], r_ov[a][r - 1])
        send(kc.at[a, :, j], kc.at[a, :, j], r_side[a][0], at_j(jr))
        send(kc.at[a, :, j], kc.at[a, :, j], r_side[a][1], at_j(jl))
        for t in range(NJ):
            jj = (j + t) % NJ
            send(kst.at[a], ko.at[a, :, j], r_oz[a] + t, at_j(jj, 1 - p))

    def gather_forward(a):
        arrived(kc.at[a, :, jl], r_side[a][0])
        send(kc.at[a, 0:2, jl], kc.at[a, 0:2, jl], r_fwd[a][0], at_j(jr))
        arrived(kc.at[a, :, jr], r_side[a][1])
        send(kc.at[a, 2:4, jr], kc.at[a, 2:4, jr], r_fwd[a][1], at_j(jl))

    def gather_end(a):
        arrived(kc.at[a, 0:2, jo], r_fwd[a][0])
        arrived(kc.at[a, 2:4, jo], r_fwd[a][1])
        for t in range(NJ):
            arrived(ko.at[a, :, (j + NJ - t) % NJ], r_oz[a] + t)

    def chunk(a, c):
        if c == 0:
            return ko[a].reshape(CHUNK, HD)
        return kc[a, c - 1].reshape(CHUNK, HD)

    gather_start(0)

    loc_x.wait()

    def turn(b, _):
        for half in range(2):
            block = xin[:, pl.ds(pl.multiple_of(b * 256 + half * 128, 128), 128)]
            xloc[b, pl.ds(half * 4, 4)] = block.T.reshape(4, 32, TOK)
        return 0

    lax.fori_loop(0, 32, turn, 0)
    r_x = take("r", 8)
    loc_xx = local(xloc.at[:, dp], xall.at[:, :, col(dp)])
    for t in range(1, NDP):
        dd = (dp + t) % NDP
        send(xloc.at[:, dd], xall.at[:, :, col(dp)], r_x + t, at_dp(dd))

    gather_forward(0)
    gather_start(1)
    loc_q.wait()
    for r in range(1, NY):
        arrived(qb.at[(y + NY - r) % NY], r_q + r)
    for r in range(1, NY):
        yy = (y + r) % NY
        send(g_ref.at[:, col(yy, ROWS)], gb.at[y], r_g + r, at_y(yy))
    gather_end(0)
    for c in range(5):
        kt[c] = chunk(0, c).T

    def heads(ref, i, hp):
        block = ref[i, :, pl.ds(pl.multiple_of(hp * 256, 256), 256)]
        return jnp.concatenate([block[:, :HD], block[:, HD:]], axis=0)

    def lanes(hp):
        return pl.ds(pl.multiple_of(hp * 256, 256), 256)

    def probs(i):
        def body(hp, _):
            qh = heads(qb, i, hp)
            top = None
            for c in range(i + 2):
                s = dot_nt(chunk(0, c), qh)
                if c == 0:
                    s = jnp.concatenate(
                        [s[n * 128:(n + 1) * 128] + bias_ref[i // 2, n] for n in range(4)], axis=0
                    )
                elif c == i + 1:
                    ahead = lax.broadcasted_iota(jnp.int32, s.shape, 0) - lax.broadcasted_iota(
                        jnp.int32, s.shape, 1
                    ) % TOK
                    s = jnp.where(ahead <= TOK * j, s, NEG)
                sbuf[c] = s
                high = jnp.max(s, axis=0, keepdims=True)
                top = high if top is None else jnp.maximum(top, high)
            total = None
            for c in range(i + 2):
                e = jnp.exp2((sbuf[c] - top) * EXPC)
                add = jnp.sum(e, axis=0, keepdims=True)
                total = add if total is None else total + add
                ebuf[UNIT[i, c], :, lanes(hp)] = e.astype(BF)
            linv[i, :, lanes(hp)] = 1.0 / total
            return 0

        lax.fori_loop(0, 4, body, 0)

    probs(0)
    probs(1)
    gather_forward(1)
    probs(2)
    probs(3)

    loc_g.wait()
    for r in range(1, NY):
        arrived(gb.at[(y + NY - r) % NY], r_g + r)

    def spread(n, _):
        i = n // 8
        h = n % 8
        at = pl.ds(pl.multiple_of(h * HD, HD), HD)
        inv = jnp.broadcast_to(linv[i, :, at], (HD, HD)).T
        gl[i, at, :] = (gb[i, :, at].astype(F32) * inv).astype(BF)
        ql[i, at, :] = (qb[i, :, at].astype(F32) * (inv * SCALE)).astype(BF)
        return 0

    lax.fori_loop(0, 32, spread, 0)

    def keys_grad(a, right):
        for c in range(5):
            first = max(c - 1, 0)
            acc = None
            for i in range(first, 4):
                term = dot(ebuf[UNIT[i, c]], right[i])
                acc = term if acc is None else acc + term
            if c == 0:
                opart[a] = acc.astype(BF).reshape(NY, NJ, OLDT, HD)
            else:
                part[a, c - 1] = acc.astype(BF).reshape(NJ, TOK, HD)

    r_m1 = [[take("r"), take("r")] for _ in range(2)]
    r_m2 = [[take("r"), take("r")] for _ in range(2)]
    r_m3 = [[take("r"), take("r")] for _ in range(2)]
    r_old = [take("r", 4) for _ in range(2)]

    def sum_start(a):
        send(part.at[a, 0:2, jo], m1.at[a, 0], r_m1[a][0], at_j(jr))
        send(part.at[a, 2:4, jo], m1.at[a, 1], r_m1[a][1], at_j(jl))
        send(part.at[a, 2:4, jr], m2.at[a, 1], r_m2[a][0], at_j(jr))
        send(part.at[a, 0:2, jl], m2.at[a, 0], r_m2[a][1], at_j(jl))
        for t in range(NJ):
            jj = (j + t) % NJ
            send(opart.at[a, :, jj], rold.at[a, t], r_old[a] + t, at_j(jj, 1 - p))

    def sum_merge(a):
        arrived(m1.at[a, 0], r_m1[a][0])
        mrg[a, 0] = (m1[a, 0].astype(F32) + part[a, 0:2, jr].astype(F32)).astype(BF)
        send(mrg.at[a, 0], m3.at[a, 0], r_m3[a][0], at_j(jr))
        arrived(m1.at[a, 1], r_m1[a][1])
        mrg[a, 1] = (m1[a, 1].astype(F32) + part[a, 2:4, jl].astype(F32)).astype(BF)
        send(mrg.at[a, 1], m3.at[a, 1], r_m3[a][1], at_j(jl))

    r_fin = [take("r", 4) for _ in range(2)]
    r_ofin = [take("r", 4) for _ in range(2)]

    def sum_end(a, here, put, oput):
        arrived(m2.at[a, 1], r_m2[a][0])
        arrived(m2.at[a, 0], r_m2[a][1])
        arrived(m3.at[a, 0], r_m3[a][0])
        arrived(m3.at[a, 1], r_m3[a][1])
        for half in range(2):
            vg4[a, pl.ds(half * 2, 2)] = (
                part[a, pl.ds(half * 2, 2), j].astype(F32)
                + m2[a, half].astype(F32)
                + m3[a, half].astype(F32)
            ).astype(BF)
        own = local(vg4.at[a, y], put)
        for r in range(1, NY):
            yy = (y + r) % NY
            send(vg4.at[a, yy], put, r_fin[a] + r, at_y(yy))
        for t in range(NJ):
            arrived(rold.at[a, t], r_old[a] + t)
        og4[a] = (
            rold[a, 0].astype(F32) + rold[a, 1].astype(F32)
            + rold[a, 2].astype(F32) + rold[a, 3].astype(F32)
        ).astype(BF)
        oown_copy = local(og4.at[a, y], oput)
        for r in range(1, NY):
            yy = (y + r) % NY
            send(og4.at[a, yy], oput, r_ofin[a] + r, at_y(yy))
        return own, oown_copy

    def sum_arrived(a, copies, whole, owhole):
        copies[0].wait()
        copies[1].wait()
        for r in range(1, NY):
            yy = (y + NY - r) % NY
            arrived(whole.at[:, col(yy)], r_fin[a] + r)
            arrived(owhole.at[:, col(yy)], r_ofin[a] + r)

    keys_grad(1, gl)
    sum_start(1)

    gather_end(1)
    r_dq = take("r", 4)

    def scores_grad(i):
        def body(hp, _):
            gh = heads(gb, i, hp)
            inv = linv[i, :, lanes(hp)]
            delta = None
            for c in range(i + 2):
                d = dot_nt(chunk(1, c), gh)
                sbuf[c] = d
                add = jnp.sum(ebuf[UNIT[i, c], :, lanes(hp)].astype(F32) * d, axis=0, keepdims=True)
                delta = add if delta is None else delta + add
            delta = delta * inv
            acc = None
            for c in range(i + 2):
                t = (ebuf[UNIT[i, c], :, lanes(hp)].astype(F32) * (sbuf[c] - delta)).astype(BF)
                ebuf[UNIT[i, c], :, lanes(hp)] = t
                term = dot(kt[c], t)
                acc = term if acc is None else acc + term
            acc = acc * (inv * SCALE)
            out = jnp.concatenate([acc[:, :HD].T, acc[:, HD:].T], axis=1)
            dqb[i, :, lanes(hp)] = out.astype(BF)
            return 0

        lax.fori_loop(0, 4, body, 0)

    scores_grad(0)
    sum_merge(1)
    scores_grad(1)
    vcopies = sum_end(1, dv_ref, vgall.at[dp, :, col(y)], odv_ref.at[:, col(y)])
    scores_grad(2)
    sum_arrived(1, vcopies, vgall.at[dp], odv_ref)
    r_vg = take("r", 4)
    r_vs = take("r", 4)
    dv_copy = local(vgall.at[dp], dv_ref)
    sib = 2 * x + 1 - core
    send(vgall.at[dp], vgall.at[dp], r_vs, at_dp(sib))
    for t in range(1, 4):
        send(vgall.at[dp], vgall.at[dp], r_vg + t, at_dp(2 * ((x + t) % 4) + core))
    scores_grad(3)
    loc_dq = local(dqb.at[y], dq_ref.at[:, col(y, ROWS)])
    for r in range(1, NY):
        yy = (y + r) % NY
        send(dqb.at[yy], dq_ref.at[:, col(y, ROWS)], r_dq + r, at_y(yy))
    for t in range(1, 4):
        d = 2 * ((x + 4 - t) % 4) + core
        arrived(vgall.at[d], r_vg + t)
        send(vgall.at[d], vgall.at[d], r_vs + t, at_dp(sib))
    keys_grad(0, ql)
    sum_start(0)

    loc_xx.wait()
    for t in range(1, NDP):
        arrived(xall.at[:, :, col((dp + NDP - t) % NDP)], r_x + t)
    for t in range(4):
        arrived(vgall.at[2 * ((x + 4 - t) % 4) + 1 - core], r_vs + t)
    r_wy = take("r", 4)

    def weight(yy):
        left = xall[pl.ds(yy * 8, 8)].reshape(256, NDP * TOK)
        return dot(left, vgall[...].reshape(NDP * TOK, 4 * HD)).reshape(8, 32, 4 * HD)

    for r in range(1, NY):
        yy = (y + r) % NY
        wp[r - 1] = weight(yy).astype(BF)
        send(wp.at[r - 1], ry.at[r - 1], r_wy + r, at_y(yy))
    sum_merge(0)
    wown[...] = weight(y)
    kcopies = sum_end(0, dk_ref, dk_ref.at[:, col(y)], odk_ref.at[:, col(y)])
    for r in range(1, NY):
        arrived(ry.at[r - 1], r_wy + r)
    wz[...] = (
        wown[...] + ry[0].astype(F32) + ry[1].astype(F32) + ry[2].astype(F32)
    ).astype(BF)
    r_wz = take("r", 8)
    for t in range(1, 8):
        zz = (z + t) % 8
        send(wz.at[zz], rz.at[t - 1], r_wz + t, at_j(zz // 2, zz % 2))
    acc = wz[z].astype(F32)
    for t in range(1, 8):
        arrived(rz.at[t - 1], r_wz + t)
        acc = acc + rz[t - 1].astype(F32)
    wfin[...] = (acc * (1.0 / 256.0)).astype(BF)
    r_wd = take("r", 8)
    rows = pl.ds(pl.multiple_of(dp * 32, 32), 32)
    own_w = local(wfin, dw_ref.at[rows])
    for t in range(1, NDP):
        send(wfin, dw_ref.at[rows], r_wd + t, at_dp((dp + t) % NDP))

    sum_arrived(0, kcopies, dk_ref, odk_ref)
    dv_copy.wait()
    loc_dq.wait()
    for r in range(1, NY):
        arrived(dq_ref.at[:, col((y + NY - r) % NY, ROWS)], r_dq + r)
    own_w.wait()
    for t in range(1, NDP):
        d = (dp + NDP - t) % NDP
        arrived(dw_ref.at[pl.ds(pl.multiple_of(d * 32, 32), 32)], r_wd + t)
    for c in sends:
        c.wait_send()
    assert count["s"] <= ssem.shape[0] and count["r"] <= rsem.shape[0]
    assert count["l"] <= lsem.shape[0]


def on_device(queries, keys, values, old_keys, old_values, out_grad, inputs, reads):
    bias = (jnp.minimum(reads[0, 0], 1).astype(F32) - 1.0) * (-NEG)
    anywhere = pl.BlockSpec(memory_space=pl.ANY)
    out = [(TOK, 4096), (TOK, 512), (TOK, 512), (OLDT, 512), (OLDT, 512), (256, 512)]
    bf = lambda *shape: pltpu.VMEM(shape, BF)
    f32 = lambda *shape: pltpu.VMEM(shape, F32)
    results = pl.pallas_call(
        kernel,
        out_shape=[jax.ShapeDtypeStruct(shape, BF) for shape in out],
        in_specs=[anywhere] * 7 + [pl.BlockSpec(memory_space=pltpu.SMEM)],
        out_specs=[anywhere] * 6,
        scratch_shapes=[
            bf(TOK, 8192),
            bf(32, 8, 32, TOK),
            bf(32, 32, NDP * TOK),
            bf(4, TOK, ROWS),
            bf(4, TOK, ROWS),
            bf(2, NY, NJ, TOK, HD),
            bf(2, NY, NJ, OLDT, HD),
            bf(2, NY, OLDT, HD),
            bf(5, HD, CHUNK),
            bf(len(UNITS), CHUNK, ROWS),
            f32(5, CHUNK, 256),
            f32(4, 1, ROWS),
            bf(4, ROWS, HD),
            bf(4, ROWS, HD),
            bf(4, TOK, ROWS),
            bf(2, NY, NJ, TOK, HD),
            bf(2, NY, NJ, OLDT, HD),
            bf(16, 128),
            bf(16, 128),
            bf(2, 2, 2, TOK, HD),
            bf(2, 2, 2, TOK, HD),
            bf(2, 2, 2, TOK, HD),
            bf(2, 2, 2, TOK, HD),
            bf(2, NJ, NY, OLDT, HD),
            bf(2, NY, TOK, HD),
            bf(2, NY, OLDT, HD),
            bf(NDP, TOK, 512),
            bf(3, 8, 32, 512),
            f32(8, 32, 512),
            bf(3, 8, 32, 512),
            bf(8, 32, 512),
            bf(7, 32, 512),
            bf(32, 512),
            pltpu.SemaphoreType.DMA((112,)),
            pltpu.SemaphoreType.DMA((128,)),
            pltpu.SemaphoreType.DMA((24,)),
        ],
        compiler_params=pltpu.CompilerParams(
            collective_id=0, has_side_effects=True, vmem_limit_bytes=56 * 1024 * 1024
        ),
        cost_estimate=pl.CostEstimate(
            flops=11_000_000_000, bytes_accessed=10_000_000, transcendentals=8_000_000
        ),
    )(
        queries[0, 0], keys[0, 0], values[0, 0], old_keys[0, 0], old_values[0, 0],
        out_grad[0, 0], inputs[0, 0], bias,
    )
    return tuple(r[None, None] for r in results[:5]) + (results[5],)


def solution(mesh):
    token = P("dp", "pool", "seq", None)
    in_specs = (token,) * 7 + (P("dp", "pool", None, None),)
    out_specs = (token,) * 5 + (P(("seq", "pool"), None),)
    return jax.shard_map(
        on_device, mesh=mesh, in_specs=in_specs, out_specs=out_specs, check_vma=False
    )
```

```python
import jax
import jax.numpy as jnp
from jax import lax
from jax.experimental import pallas as pl
from jax.experimental.pallas import tpu as pltpu
from jax.sharding import PartitionSpec as P

MESH = pl.DeviceIdType.MESH
BF = jnp.bfloat16
F32 = jnp.float32
HD = 128
NY = 4
NJ = 4
NDP = 8
TOK = 128
OLDT = 32
ROWS = 1024
CHUNK = 512
SCALE = HD**-0.5
EXPC = SCALE * 1.4426950408889634
NEG = -1e30
SENDS, RECVS = 180, 220
UNITS = [(i, c) for i in range(4) for c in range(i + 2)]
UNIT = {u: n for n, u in enumerate(UNITS)}


def dot(a, b):
    return jnp.dot(a, b, preferred_element_type=F32)


def dot_nt(a, b):
    return lax.dot_general(a, b, (((1,), (1,)), ((), ())), preferred_element_type=F32)


def kernel(
    q_ref, k_ref, v_ref, ok_ref, ov_ref, g_ref, x_ref, reads_ref,
    dq_ref, dk_ref, dv_ref, odk_ref, odv_ref, dw_ref,
    xin, xloc, xall, qb, gb, kc, ko, kst, kt, ebuf, sbuf, linv, lcol, gl, ql, dqb,
    vacc, part, opart, m1, m2, m3, mrg, rold, vg4, og4, vgall,
    wp, wown, ry, wz, rz, wfin, ssem, rsem, lsem,
):
    seq = lax.axis_index("seq")
    p = lax.axis_index("pool")
    dp = lax.axis_index("dp")
    y = seq // NJ
    j = seq % NJ
    z = 2 * j + p
    x = dp // 2
    core = dp % 2
    jr = (j + 1) % NJ
    jl = (j + 3) % NJ
    jo = (j + 2) % NJ

    def at_y(yy):
        return (yy * NJ + j, p, dp)

    def at_j(jj, pp=None):
        return (y * NJ + jj, p if pp is None else pp, dp)

    def at_dp(dd):
        return (seq, p, dd)

    count = {"s": 0, "r": 0, "l": 0}
    sends = []

    def take(kind, n=1):
        base = count[kind]
        count[kind] += n
        return base

    def send(src, dst, rs, dev):
        c = pltpu.make_async_remote_copy(
            src_ref=src, dst_ref=dst, send_sem=ssem.at[take("s")], recv_sem=rsem.at[rs],
            device_id=dev, device_id_type=MESH,
        )
        c.start()
        sends.append(c)

    def arrived(dst, rs):
        pltpu.make_async_copy(dst, dst, rsem.at[rs]).wait()

    def local(src, dst):
        c = pltpu.make_async_copy(src, dst, lsem.at[take("l")])
        c.start()
        return c

    barrier = pltpu.get_barrier_semaphore()
    peers = [at_y((y + r) % NY) for r in range(1, NY)]
    peers += [at_j(((z + t) % 8) // 2, ((z + t) % 8) % 2) for t in range(1, 8)]
    peers += [at_dp((dp + t) % NDP) for t in range(1, NDP)]
    for dev in peers:
        pl.semaphore_signal(barrier, inc=1, device_id=dev, device_id_type=MESH)
    pl.semaphore_wait(barrier, len(peers))

    def col(n, width=HD):
        return pl.ds(pl.multiple_of(n * width, width), width)

    def lanes(hp):
        return pl.ds(hp * 256, 256)

    def quarter(n, hp):
        return pl.ds(pl.multiple_of(n * ROWS + hp * 256, 256), 256)

    r_kv = [[take("r") for _ in range(3)] for _ in range(2)]
    r_ov = [[take("r") for _ in range(3)] for _ in range(2)]
    r_q = [take("r", 4) for _ in range(4)]
    r_g = [take("r", 4) for _ in range(4)]
    loc_kv = []

    def send_kv(a, cur, old):
        for r in range(1, NY):
            yy = (y + r) % NY
            send(cur.at[:, col(yy)], kc.at[a, y, j], r_kv[a][r - 1], at_y(yy))
            send(old.at[:, col(yy)], kst.at[a, y], r_ov[a][r - 1], at_y(yy))
        loc_kv.append(
            (local(cur.at[:, col(y)], kc.at[a, y, j]), local(old.at[:, col(y)], kst.at[a, y]))
        )

    def send_rows(ref, buf, base, hp):
        for r in (2, 1, 3):
            yy = (y + r) % NY
            send(ref.at[:, quarter(yy, hp)], buf.at[y, :, lanes(hp)], base[hp] + r, at_y(yy))

    def rows_arrived(buf, base, hp):
        for r in range(1, NY):
            arrived(buf.at[(y + NY - r) % NY, :, lanes(hp)], base[hp] + r)

    send_kv(0, k_ref, ok_ref)
    send_rows(q_ref, qb, r_q, 0)
    loc_x = local(x_ref, xin)
    loc_q = local(q_ref.at[:, col(y, ROWS)], qb.at[y])
    loc_g = local(g_ref.at[:, col(y, ROWS)], gb.at[y])

    r_side = [[take("r", 2), take("r", 2)] for _ in range(2)]
    r_fwd = [[take("r"), take("r")] for _ in range(2)]
    r_oz = [take("r", 4) for _ in range(2)]

    def gather_start(a):
        loc_kv[a][0].wait()
        loc_kv[a][1].wait()
        for r in range(1, NY):
            yy = (y + NY - r) % NY
            arrived(kc.at[a, yy, j], r_kv[a][r - 1])
            arrived(kst.at[a, yy], r_ov[a][r - 1])
        low, high = kc.at[a, 0:2, j], kc.at[a, 2:4, j]
        send(low, low, r_side[a][0], at_j(jr))
        send(high, high, r_side[a][1], at_j(jl))
        send(high, high, r_side[a][0] + 1, at_j(jr))
        send(low, low, r_side[a][1] + 1, at_j(jl))

    def gather_forward(a):
        arrived(kc.at[a, 0:2, jl], r_side[a][0])
        send(kc.at[a, 0:2, jl], kc.at[a, 0:2, jl], r_fwd[a][0], at_j(jr))
        arrived(kc.at[a, 2:4, jr], r_side[a][1])
        send(kc.at[a, 2:4, jr], kc.at[a, 2:4, jr], r_fwd[a][1], at_j(jl))
        for t in range(NJ):
            jj = (j + t) % NJ
            send(kst.at[a], ko.at[a, :, j], r_oz[a] + t, at_j(jj, 1 - p))

    def gather_end(a):
        arrived(kc.at[a, 2:4, jl], r_side[a][0] + 1)
        arrived(kc.at[a, 0:2, jr], r_side[a][1] + 1)
        arrived(kc.at[a, 0:2, jo], r_fwd[a][0])
        arrived(kc.at[a, 2:4, jo], r_fwd[a][1])
        for t in range(NJ):
            arrived(ko.at[a, :, (j + NJ - t) % NJ], r_oz[a] + t)

    def chunk(a, c):
        if c == 0:
            return ko[a].reshape(CHUNK, HD)
        return kc[a, c - 1].reshape(CHUNK, HD)

    gather_start(0)
    for hp in range(1, 4):
        send_rows(q_ref, qb, r_q, hp)

    loc_x.wait()

    def turn(b, _):
        for half in range(2):
            block = xin[:, pl.ds(pl.multiple_of(b * 256 + half * 128, 128), 128)]
            xloc[b, pl.ds(half * 4, 4)] = block.T.reshape(4, 32, TOK)
        return 0

    lax.fori_loop(0, 32, turn, 0, unroll=4)
    r_x = take("r", 8)
    loc_xx = local(xloc.at[:, dp], xall.at[:, :, col(dp)])
    for t in range(1, NDP):
        dd = (dp + t) % NDP
        send(xloc.at[:, dd], xall.at[:, :, col(dp)], r_x + t, at_dp(dd))

    gather_forward(0)
    send_kv(1, v_ref, ov_ref)
    for hp in range(4):
        rows_arrived(qb, r_q, hp)
    for hp in range(4):
        send_rows(g_ref, gb, r_g, hp)
    loc_q.wait()
    gather_end(0)
    for c in range(5):
        kt[c] = chunk(0, c).T
    gather_start(1)

    def heads(ref, i, hp):
        block = ref[i, :, lanes(hp)]
        return jnp.concatenate([block[:, :HD], block[:, HD:]], axis=0)

    bias = [
        [(jnp.minimum(reads_ref[s, n], 1) - 1).astype(F32) * (-NEG) for n in range(4)]
        for s in range(2)
    ]

    def probs(hp, i):
        qh = heads(qb, i, hp)
        top = None
        slot = i % 2
        for c in range(i + 2):
            s = dot_nt(chunk(0, c), qh)
            if c == 0:
                s = jnp.concatenate(
                    [s[n * 128:(n + 1) * 128] + bias[i // 2][n] for n in range(4)], axis=0
                )
            elif c == i + 1:
                ahead = lax.broadcasted_iota(jnp.int32, s.shape, 0) - lax.broadcasted_iota(
                    jnp.int32, s.shape, 1
                ) % TOK
                s = jnp.where(ahead <= TOK * j, s, NEG)
            sbuf[slot, c] = s
            high = jnp.max(s, axis=0, keepdims=True)
            top = high if top is None else jnp.maximum(top, high)
        total = None
        for c in range(i + 2):
            e = jnp.exp2((sbuf[slot, c] - top) * EXPC)
            add = jnp.sum(e, axis=0, keepdims=True)
            total = add if total is None else total + add
            ebuf[UNIT[i, c], :, lanes(hp)] = e.astype(BF)
        linv[i, :, lanes(hp)] = 1.0 / total

    for hp in range(4):
        for i in range(4):
            probs(hp, i)
        if hp == 1:
            gather_forward(1)

    def spread(hp):
        for i in range(4):
            for h in (2 * hp, 2 * hp + 1):
                at = pl.ds(h * HD, HD)
                inv = jnp.broadcast_to(linv[i, :, at], (HD, HD)).T
                lcol[i, at, :] = inv
                gl[i, at, :] = (gb[i, :, at].astype(F32) * inv).astype(BF)

    def spread_q(n, _):
        i = n // 8
        h = n % 8
        at = pl.ds(pl.multiple_of(h * HD, HD), HD)
        ql[i, at, :] = (qb[i, :, at].astype(F32) * (lcol[i, at, :] * SCALE)).astype(BF)
        return 0

    def keys_grad(right, c, rows=slice(None)):
        acc = None
        for i in range(max(c - 1, 0), 4):
            term = dot(ebuf[UNIT[i, c], :, rows], right[i, rows])
            acc = term if acc is None else acc + term
        return acc

    def keep(a, c, acc):
        if c == 0:
            opart[a] = acc.astype(BF).reshape(NY, NJ, OLDT, HD)
        else:
            part[a, c - 1] = acc.astype(BF).reshape(NJ, TOK, HD)

    r_m1 = [[take("r"), take("r")] for _ in range(2)]
    r_m2 = [[take("r"), take("r")] for _ in range(2)]
    r_m3 = [[take("r"), take("r")] for _ in range(2)]
    r_old = [take("r", 4) for _ in range(2)]

    def sum_low(a):
        send(part.at[a, 0:2, jo], m1.at[a, 0], r_m1[a][0], at_j(jr))
        send(part.at[a, 0:2, jl], m2.at[a, 0], r_m2[a][1], at_j(jl))

    def sum_high(a):
        send(part.at[a, 2:4, jo], m1.at[a, 1], r_m1[a][1], at_j(jl))
        send(part.at[a, 2:4, jr], m2.at[a, 1], r_m2[a][0], at_j(jr))

    def sum_merge(a):
        arrived(m1.at[a, 0], r_m1[a][0])
        mrg[a, 0] = (m1[a, 0].astype(F32) + part[a, 0:2, jr].astype(F32)).astype(BF)
        send(mrg.at[a, 0], m3.at[a, 0], r_m3[a][0], at_j(jr))
        arrived(m1.at[a, 1], r_m1[a][1])
        mrg[a, 1] = (m1[a, 1].astype(F32) + part[a, 2:4, jl].astype(F32)).astype(BF)
        send(mrg.at[a, 1], m3.at[a, 1], r_m3[a][1], at_j(jl))
        for t in range(NJ):
            jj = (j + t) % NJ
            send(opart.at[a, :, jj], rold.at[a, t], r_old[a] + t, at_j(jj, 1 - p))

    r_fin = [take("r", 4) for _ in range(2)]
    r_ofin = [take("r", 4) for _ in range(2)]

    def sum_end(a, put):
        arrived(m2.at[a, 1], r_m2[a][0])
        arrived(m2.at[a, 0], r_m2[a][1])
        arrived(m3.at[a, 0], r_m3[a][0])
        arrived(m3.at[a, 1], r_m3[a][1])
        for half in range(2):
            vg4[a, pl.ds(half * 2, 2)] = (
                part[a, pl.ds(half * 2, 2), j].astype(F32)
                + m2[a, half].astype(F32)
                + m3[a, half].astype(F32)
            ).astype(BF)
        own = local(vg4.at[a, y], put)
        for r in range(1, NY):
            yy = (y + r) % NY
            send(vg4.at[a, yy], put, r_fin[a] + r, at_y(yy))
        return own

    def sum_old(a, oput):
        for t in range(NJ):
            arrived(rold.at[a, t], r_old[a] + t)
        og4[a] = (
            rold[a, 0].astype(F32) + rold[a, 1].astype(F32)
            + rold[a, 2].astype(F32) + rold[a, 3].astype(F32)
        ).astype(BF)
        oown_copy = local(og4.at[a, y], oput)
        for r in range(1, NY):
            yy = (y + r) % NY
            send(og4.at[a, yy], oput, r_ofin[a] + r, at_y(yy))
        return oown_copy

    def by_head(copy, base, whole):
        copy.wait()
        for r in range(1, NY):
            arrived(whole.at[:, col((y + NY - r) % NY)], base + r)

    loc_g.wait()
    first, second = pl.ds(0, 512), pl.ds(512, 512)
    for hp in range(2):
        rows_arrived(gb, r_g, hp)
        spread(hp)
    for c in range(5):
        vacc[c] = keys_grad(gl, c, first)
    for hp in range(2, 4):
        rows_arrived(gb, r_g, hp)
        spread(hp)
    for c in (1, 2, 3, 4, 0):
        keep(1, c, vacc[c] + keys_grad(gl, c, second))
        if c == 2:
            sum_low(1)
        if c == 4:
            sum_high(1)

    gather_end(1)
    r_dq = [take("r", 4) for _ in range(4)]

    def scores_grad(hp, i):
        gh = heads(gb, i, hp)
        inv = linv[i, :, lanes(hp)]
        slot = i % 2
        delta = None
        for c in range(i + 2):
            d = dot_nt(chunk(1, c), gh)
            sbuf[slot, c] = d
            add = jnp.sum(ebuf[UNIT[i, c], :, lanes(hp)].astype(F32) * d, axis=0, keepdims=True)
            delta = add if delta is None else delta + add
        delta = delta * inv
        acc = None
        for c in range(i + 2):
            t = (ebuf[UNIT[i, c], :, lanes(hp)].astype(F32) * (sbuf[slot, c] - delta)).astype(BF)
            ebuf[UNIT[i, c], :, lanes(hp)] = t
            term = dot(kt[c], t)
            acc = term if acc is None else acc + term
        acc = acc * (inv * SCALE)
        out = jnp.concatenate([acc[:, :HD].T, acc[:, HD:].T], axis=1)
        dqb[i, :, lanes(hp)] = out.astype(BF)

    loc_dq = []

    def send_dq(hp):
        loc_dq.append(local(dqb.at[y, :, lanes(hp)], dq_ref.at[:, quarter(y, hp)]))
        for r in range(1, NY):
            yy = (y + r) % NY
            send(dqb.at[yy, :, lanes(hp)], dq_ref.at[:, quarter(y, hp)], r_dq[hp] + r, at_y(yy))

    for i in range(4):
        scores_grad(0, i)
    send_dq(0)
    scores_grad(1, 0)
    sum_merge(1)
    for i in range(1, 4):
        scores_grad(1, i)
    send_dq(1)
    v_own = sum_end(1, vgall.at[dp, :, col(y)])
    for i in range(4):
        scores_grad(2, i)
    send_dq(2)
    r_vg = take("r", 4)
    r_vs = take("r", 4)
    by_head(v_own, r_fin[1], vgall.at[dp])
    sib = 2 * x + 1 - core
    for t in (1, 3, 2):
        send(vgall.at[dp], vgall.at[dp], r_vg + t, at_dp(2 * ((x + t) % 4) + core))
    send(vgall.at[dp], vgall.at[dp], r_vs, at_dp(sib))
    dv_copy = local(vgall.at[dp], dv_ref)
    for i in range(4):
        scores_grad(3, i)
    send_dq(3)
    ov_own = sum_old(1, odv_ref.at[:, col(y)])
    lax.fori_loop(0, 32, spread_q, 0, unroll=8)
    for c in (1, 2):
        keep(0, c, keys_grad(ql, c))
    sum_low(0)
    for t in (1, 3, 2):
        d = 2 * ((x + 4 - t) % 4) + core
        arrived(vgall.at[d], r_vg + t)
        send(vgall.at[d], vgall.at[d], r_vs + t, at_dp(sib))

    loc_xx.wait()
    for t in range(1, NDP):
        arrived(xall.at[:, :, col((dp + NDP - t) % NDP)], r_x + t)
    for c in (3, 4):
        keep(0, c, keys_grad(ql, c))
    sum_high(0)
    for t in range(4):
        arrived(vgall.at[2 * ((x + 4 - t) % 4) + 1 - core], r_vs + t)
    r_wy = [take("r", 4), take("r", 4)]

    def weight(yy):
        left = xall[pl.ds(yy * 8, 8)].reshape(256, NDP * TOK)
        return dot(left, vgall[...].reshape(NDP * TOK, 4 * HD)).reshape(8, 32, 4 * HD)

    for r in (2, 1, 3):
        yy = (y + r) % NY
        both = weight(yy).astype(BF)
        wp[r - 1, 0] = both[:, :16]
        wp[r - 1, 1] = both[:, 16:]
        send(wp.at[r - 1, 0], ry.at[r - 1, 0], r_wy[0] + r, at_y(yy))
    for r in (2, 1, 3):
        send(wp.at[r - 1, 1], ry.at[r - 1, 1], r_wy[1] + r, at_y((y + r) % NY))
    keep(0, 0, keys_grad(ql, 0))
    sum_merge(0)
    both = weight(y)
    wown[0] = both[:, :16]
    wown[1] = both[:, 16:]
    r_wz = [take("r", 8), take("r", 8)]
    r_wd = [take("r", 8), take("r", 8)]

    def weight_y(h):
        for r in range(1, NY):
            arrived(ry.at[r - 1, h], r_wy[h] + r)
        wz[h] = (
            wown[h] + ry[0, h].astype(F32) + ry[1, h].astype(F32) + ry[2, h].astype(F32)
        ).astype(BF)
        for t in (4, 3, 5, 2, 6, 1, 7):
            zz = (z + t) % 8
            send(wz.at[h, zz], rz.at[t - 1, h], r_wz[h] + t, at_j(zz // 2, zz % 2))

    def rows(d, h):
        return pl.ds(pl.multiple_of(d * 32 + h * 16, 16), 16)

    def weight_z(h):
        acc = wz[h, z].astype(F32)
        for t in range(1, 8):
            arrived(rz.at[t - 1, h], r_wz[h] + t)
            acc = acc + rz[t - 1, h].astype(F32)
        wfin[h] = (acc * (1.0 / 256.0)).astype(BF)
        own = local(wfin.at[h], dw_ref.at[rows(dp, h)])
        for t in (4, 3, 5, 2, 6, 1, 7):
            send(wfin.at[h], dw_ref.at[rows(dp, h)], r_wd[h] + t, at_dp((dp + t) % NDP))
        return own

    weight_y(0)
    k_own = sum_end(0, dk_ref.at[:, col(y)])
    weight_y(1)
    ok_own = sum_old(0, odk_ref.at[:, col(y)])
    own_w = [weight_z(0), weight_z(1)]

    by_head(k_own, r_fin[0], dk_ref)
    by_head(ok_own, r_ofin[0], odk_ref)
    by_head(ov_own, r_ofin[1], odv_ref)
    dv_copy.wait()
    for hp in range(4):
        loc_dq[hp].wait()
        for r in range(1, NY):
            arrived(dq_ref.at[:, quarter((y + NY - r) % NY, hp)], r_dq[hp] + r)
    for h in range(2):
        own_w[h].wait()
        for t in range(1, NDP):
            arrived(dw_ref.at[rows((dp + NDP - t) % NDP, h)], r_wd[h] + t)
    for c in sends:
        c.wait_send()
    assert count["s"] <= ssem.shape[0] and count["r"] <= rsem.shape[0]
    assert count["l"] <= lsem.shape[0]


def deliver(*refs):
    source, target, held = refs[:6], refs[6:12], refs[12:18]
    sem_in, sem_out = refs[18:]
    inward = [pltpu.make_async_copy(source[n], held[n], sem_in.at[n]) for n in range(6)]
    outward = [pltpu.make_async_copy(held[n], target[n], sem_out.at[n]) for n in range(6)]
    for c in inward:
        c.start()
    for n in range(6):
        inward[n].wait()
        outward[n].start()
    for c in outward:
        c.wait()


def on_device(queries, keys, values, old_keys, old_values, out_grad, inputs, reads):
    anywhere = pl.BlockSpec(memory_space=pl.ANY)
    out = [(TOK, 4096), (TOK, 512), (TOK, 512), (OLDT, 512), (OLDT, 512), (256, 512)]
    bf = lambda *shape: pltpu.VMEM(shape, BF)
    f32 = lambda *shape: pltpu.VMEM(shape, F32)
    results = pl.pallas_call(
        kernel,
        out_shape=[jax.ShapeDtypeStruct(shape, BF) for shape in out],
        in_specs=[anywhere] * 7 + [pl.BlockSpec(memory_space=pltpu.SMEM)],
        out_specs=[anywhere] * 6,
        scratch_shapes=[
            bf(TOK, 8192),
            bf(32, 8, 32, TOK),
            bf(32, 32, NDP * TOK),
            bf(4, TOK, ROWS),
            bf(4, TOK, ROWS),
            bf(2, NY, NJ, TOK, HD),
            bf(2, NY, NJ, OLDT, HD),
            bf(2, NY, OLDT, HD),
            bf(5, HD, CHUNK),
            bf(len(UNITS), CHUNK, ROWS),
            f32(2, 5, CHUNK, 256),
            f32(4, 1, ROWS),
            f32(4, ROWS, HD),
            bf(4, ROWS, HD),
            bf(4, ROWS, HD),
            bf(4, TOK, ROWS),
            f32(5, CHUNK, HD),
            bf(2, NY, NJ, TOK, HD),
            bf(2, NY, NJ, OLDT, HD),
            bf(2, 2, 2, TOK, HD),
            bf(2, 2, 2, TOK, HD),
            bf(2, 2, 2, TOK, HD),
            bf(2, 2, 2, TOK, HD),
            bf(2, NJ, NY, OLDT, HD),
            bf(2, NY, TOK, HD),
            bf(2, NY, OLDT, HD),
            bf(NDP, TOK, 512),
            bf(3, 2, 8, 16, 512),
            f32(2, 8, 16, 512),
            bf(3, 2, 8, 16, 512),
            bf(2, 8, 16, 512),
            bf(7, 2, 16, 512),
            bf(2, 16, 512),
            pltpu.SemaphoreType.DMA((SENDS,)),
            pltpu.SemaphoreType.DMA((RECVS,)),
            pltpu.SemaphoreType.DMA((24,)),
        ],
        compiler_params=pltpu.CompilerParams(
            collective_id=0, has_side_effects=True, vmem_limit_bytes=56 * 1024 * 1024
        ),
        cost_estimate=pl.CostEstimate(
            flops=11_000_000_000, bytes_accessed=10_000_000, transcendentals=8_000_000
        ),
    )(
        queries[0, 0], keys[0, 0], values[0, 0], old_keys[0, 0], old_values[0, 0],
        out_grad[0, 0], inputs[0, 0], reads[0, 0],
    )
    results = pl.pallas_call(
        deliver,
        out_shape=[jax.ShapeDtypeStruct(shape, BF) for shape in out],
        in_specs=[anywhere] * 6,
        out_specs=[anywhere] * 6,
        scratch_shapes=[bf(*shape) for shape in out]
        + [pltpu.SemaphoreType.DMA((6,)), pltpu.SemaphoreType.DMA((6,))],
    )(*results)
    return tuple(r[None, None] for r in results[:5]) + (results[5],)


def solution(mesh):
    token = P("dp", "pool", "seq", None)
    in_specs = (token,) * 7 + (P("dp", "pool", None, None),)
    out_specs = (token,) * 5 + (P(("seq", "pool"), None),)
    return jax.shard_map(
        on_device, mesh=mesh, in_specs=in_specs, out_specs=out_specs, check_vma=False
    )
```

```python
import jax
import jax.numpy as jnp
from jax import lax
from jax.experimental import pallas as pl
from jax.experimental.pallas import tpu as pltpu
from jax.sharding import PartitionSpec as P

MESH = pl.DeviceIdType.MESH
BF = jnp.bfloat16
F32 = jnp.float32
HD = 128
NY = 4
NJ = 4
NDP = 8
TOK = 128
OLDT = 32
ROWS = 1024
CHUNK = 512
SCALE = HD**-0.5
EXPC = SCALE * 1.4426950408889634
NEG = -1e30
SENDS, RECVS = 180, 220
UNITS = [(i, c) for i in range(4) for c in range(i + 2)]
UNIT = {u: n for n, u in enumerate(UNITS)}


def dot(a, b):
    return jnp.dot(a, b, preferred_element_type=F32)


def dot_nt(a, b):
    return lax.dot_general(a, b, (((1,), (1,)), ((), ())), preferred_element_type=F32)


def kernel(
    q_ref, k_ref, v_ref, ok_ref, ov_ref, g_ref, x_ref, reads_ref,
    dq_ref, dk_ref, dv_ref, odk_ref, odv_ref, dw_ref,
    xin, xloc, xall, qb, gb, kc, ko, kst, kt, ebuf, sbuf, linv, lcol, gl, ql, dqb,
    vacc, part, opart, m1, m2, m3, mrg, rold, vg4, og4, vgall,
    wp, wown, ry, wz, rz, wfin, ssem, rsem, lsem,
):
    seq = lax.axis_index("seq")
    p = lax.axis_index("pool")
    dp = lax.axis_index("dp")
    y = seq // NJ
    j = seq % NJ
    z = 2 * j + p
    x = dp // 2
    core = dp % 2
    jr = (j + 1) % NJ
    jl = (j + 3) % NJ
    jo = (j + 2) % NJ

    def at_y(yy):
        return (yy * NJ + j, p, dp)

    def at_j(jj, pp=None):
        return (y * NJ + jj, p if pp is None else pp, dp)

    def at_dp(dd):
        return (seq, p, dd)

    count = {"s": 0, "r": 0, "l": 0}
    sends = []

    def take(kind, n=1):
        base = count[kind]
        count[kind] += n
        return base

    def send(src, dst, rs, dev):
        c = pltpu.make_async_remote_copy(
            src_ref=src, dst_ref=dst, send_sem=ssem.at[take("s")], recv_sem=rsem.at[rs],
            device_id=dev, device_id_type=MESH,
        )
        c.start()
        sends.append(c)

    def arrived(dst, rs):
        pltpu.make_async_copy(dst, dst, rsem.at[rs]).wait()

    def local(src, dst):
        c = pltpu.make_async_copy(src, dst, lsem.at[take("l")])
        c.start()
        return c

    barrier = pltpu.get_barrier_semaphore()
    peers = [at_y((y + r) % NY) for r in range(1, NY)]
    peers += [at_j(((z + t) % 8) // 2, ((z + t) % 8) % 2) for t in range(1, 8)]
    peers += [at_dp((dp + t) % NDP) for t in range(1, NDP)]
    for dev in peers:
        pl.semaphore_signal(barrier, inc=1, device_id=dev, device_id_type=MESH)
    pl.semaphore_wait(barrier, len(peers))

    def col(n, width=HD):
        return pl.ds(pl.multiple_of(n * width, width), width)

    def lanes(hp):
        return pl.ds(hp * 256, 256)

    def quarter(n, hp):
        return pl.ds(pl.multiple_of(n * ROWS + hp * 256, 256), 256)

    def half_of(n, hp):
        return pl.ds(pl.multiple_of(n * ROWS + hp * 256, 512), 512)

    r_kv = [[take("r") for _ in range(3)] for _ in range(2)]
    r_ov = [[take("r") for _ in range(3)] for _ in range(2)]
    r_q = [take("r", 4) for _ in range(4)]
    r_g = [take("r", 4) for _ in range(4)]
    loc_kv = []

    def send_kv(a, cur, old):
        for r in range(1, NY):
            yy = (y + r) % NY
            send(cur.at[:, col(yy)], kc.at[a, y, j], r_kv[a][r - 1], at_y(yy))
            send(old.at[:, col(yy)], kst.at[a, y], r_ov[a][r - 1], at_y(yy))
        loc_kv.append(
            (local(cur.at[:, col(y)], kc.at[a, y, j]), local(old.at[:, col(y)], kst.at[a, y]))
        )

    def send_rows(ref, buf, base, hp):
        for r in (2, 1, 3):
            yy = (y + r) % NY
            send(ref.at[:, quarter(yy, hp)], buf.at[y, :, lanes(hp)], base[hp] + r, at_y(yy))

    def rows_arrived(buf, base, hp):
        for r in range(1, NY):
            arrived(buf.at[(y + NY - r) % NY, :, lanes(hp)], base[hp] + r)

    send_kv(0, k_ref, ok_ref)
    send_rows(q_ref, qb, r_q, 0)
    loc_x = local(x_ref, xin)
    loc_q = local(q_ref.at[:, col(y, ROWS)], qb.at[y])
    loc_g = local(g_ref.at[:, col(y, ROWS)], gb.at[y])

    r_side = [[take("r", 2), take("r", 2)] for _ in range(2)]
    r_fwd = [[take("r"), take("r")] for _ in range(2)]
    r_oz = [take("r", 4) for _ in range(2)]

    def gather_start(a):
        loc_kv[a][0].wait()
        loc_kv[a][1].wait()
        for r in range(1, NY):
            yy = (y + NY - r) % NY
            arrived(kc.at[a, yy, j], r_kv[a][r - 1])
            arrived(kst.at[a, yy], r_ov[a][r - 1])
        low, high = kc.at[a, 0:2, j], kc.at[a, 2:4, j]
        send(low, low, r_side[a][0], at_j(jr))
        send(high, high, r_side[a][1], at_j(jl))
        send(high, high, r_side[a][0] + 1, at_j(jr))
        send(low, low, r_side[a][1] + 1, at_j(jl))

    def gather_forward(a):
        arrived(kc.at[a, 0:2, jl], r_side[a][0])
        send(kc.at[a, 0:2, jl], kc.at[a, 0:2, jl], r_fwd[a][0], at_j(jr))
        arrived(kc.at[a, 2:4, jr], r_side[a][1])
        send(kc.at[a, 2:4, jr], kc.at[a, 2:4, jr], r_fwd[a][1], at_j(jl))
        for t in range(NJ):
            jj = (j + t) % NJ
            send(kst.at[a], ko.at[a, :, j], r_oz[a] + t, at_j(jj, 1 - p))

    def gather_end(a):
        arrived(kc.at[a, 2:4, jl], r_side[a][0] + 1)
        arrived(kc.at[a, 0:2, jr], r_side[a][1] + 1)
        arrived(kc.at[a, 0:2, jo], r_fwd[a][0])
        arrived(kc.at[a, 2:4, jo], r_fwd[a][1])
        for t in range(NJ):
            arrived(ko.at[a, :, (j + NJ - t) % NJ], r_oz[a] + t)

    def chunk(a, c):
        if c == 0:
            return ko[a].reshape(CHUNK, HD)
        return kc[a, c - 1].reshape(CHUNK, HD)

    gather_start(0)
    for hp in range(1, 4):
        send_rows(q_ref, qb, r_q, hp)

    gather_forward(0)
    send_kv(1, v_ref, ov_ref)

    loc_x.wait()

    def turn(b, _):
        for half in range(2):
            block = xin[:, pl.ds(pl.multiple_of(b * 256 + half * 128, 128), 128)]
            xloc[b, pl.ds(half * 4, 4)] = block.T.reshape(4, 32, TOK)
        return 0

    lax.fori_loop(0, 32, turn, 0, unroll=4)
    r_x = take("r", 8)
    loc_xx = local(xloc.at[:, dp], xall.at[:, :, col(dp)])
    for t in range(1, NDP):
        dd = (dp + t) % NDP
        send(xloc.at[:, dd], xall.at[:, :, col(dp)], r_x + t, at_dp(dd))

    for hp in range(4):
        rows_arrived(qb, r_q, hp)
    for hp in range(4):
        send_rows(g_ref, gb, r_g, hp)
    loc_q.wait()
    gather_end(0)
    for c in range(5):
        kt[c] = chunk(0, c).T
    gather_start(1)

    def heads(ref, i, hp):
        block = ref[i, :, lanes(hp)]
        return jnp.concatenate([block[:, :HD], block[:, HD:]], axis=0)

    bias = [
        [(jnp.minimum(reads_ref[s, n], 1) - 1).astype(F32) * (-NEG) for n in range(4)]
        for s in range(2)
    ]

    def probs(hp, i):
        qh = heads(qb, i, hp)
        top = None
        slot = i % 2
        for c in range(i + 2):
            s = dot_nt(chunk(0, c), qh)
            if c == 0:
                s = jnp.concatenate(
                    [s[n * 128:(n + 1) * 128] + bias[i // 2][n] for n in range(4)], axis=0
                )
            elif c == i + 1:
                ahead = lax.broadcasted_iota(jnp.int32, s.shape, 0) - lax.broadcasted_iota(
                    jnp.int32, s.shape, 1
                ) % TOK
                s = jnp.where(ahead <= TOK * j, s, NEG)
            sbuf[slot, c] = s
            high = jnp.max(s, axis=0, keepdims=True)
            top = high if top is None else jnp.maximum(top, high)
        total = None
        for c in range(i + 2):
            e = jnp.exp2((sbuf[slot, c] - top) * EXPC)
            add = jnp.sum(e, axis=0, keepdims=True)
            total = add if total is None else total + add
            ebuf[UNIT[i, c], :, lanes(hp)] = e.astype(BF)
        linv[i, :, lanes(hp)] = 1.0 / total

    for hp in range(4):
        for i in range(4):
            probs(hp, i)
        if hp == 1:
            gather_forward(1)

    def spread(hp):
        for i in range(4):
            for h in (2 * hp, 2 * hp + 1):
                at = pl.ds(h * HD, HD)
                inv = jnp.broadcast_to(linv[i, :, at], (HD, HD)).T
                lcol[i, at, :] = inv
                gl[i, at, :] = (gb[i, :, at].astype(F32) * inv).astype(BF)

    def spread_q(n, _):
        i = n // 8
        h = n % 8
        at = pl.ds(pl.multiple_of(h * HD, HD), HD)
        ql[i, at, :] = (qb[i, :, at].astype(F32) * (lcol[i, at, :] * SCALE)).astype(BF)
        return 0

    def keys_grad(right, c, rows=slice(None)):
        acc = None
        for i in range(max(c - 1, 0), 4):
            term = dot(ebuf[UNIT[i, c], :, rows], right[i, rows])
            acc = term if acc is None else acc + term
        return acc

    def keep(a, c, acc):
        if c == 0:
            opart[a] = acc.astype(BF).reshape(NY, NJ, OLDT, HD)
        else:
            part[a, c - 1] = acc.astype(BF).reshape(NJ, TOK, HD)

    r_m1 = [[take("r"), take("r")] for _ in range(2)]
    r_m2 = [[take("r"), take("r")] for _ in range(2)]
    r_m3 = [[take("r"), take("r")] for _ in range(2)]
    r_old = [take("r", 4) for _ in range(2)]

    def sum_low(a):
        send(part.at[a, 0:2, jo], m1.at[a, 0], r_m1[a][0], at_j(jr))
        send(part.at[a, 0:2, jl], m2.at[a, 0], r_m2[a][1], at_j(jl))

    def sum_high(a):
        send(part.at[a, 2:4, jo], m1.at[a, 1], r_m1[a][1], at_j(jl))
        send(part.at[a, 2:4, jr], m2.at[a, 1], r_m2[a][0], at_j(jr))

    def sum_merge(a):
        arrived(m1.at[a, 0], r_m1[a][0])
        mrg[a, 0] = (m1[a, 0].astype(F32) + part[a, 0:2, jr].astype(F32)).astype(BF)
        send(mrg.at[a, 0], m3.at[a, 0], r_m3[a][0], at_j(jr))
        arrived(m1.at[a, 1], r_m1[a][1])
        mrg[a, 1] = (m1[a, 1].astype(F32) + part[a, 2:4, jl].astype(F32)).astype(BF)
        send(mrg.at[a, 1], m3.at[a, 1], r_m3[a][1], at_j(jl))
        for t in range(NJ):
            jj = (j + t) % NJ
            send(opart.at[a, :, jj], rold.at[a, t], r_old[a] + t, at_j(jj, 1 - p))

    r_fin = [take("r", 4) for _ in range(2)]
    r_ofin = [take("r", 4) for _ in range(2)]

    def sum_end(a, put):
        arrived(m2.at[a, 1], r_m2[a][0])
        arrived(m2.at[a, 0], r_m2[a][1])
        arrived(m3.at[a, 0], r_m3[a][0])
        arrived(m3.at[a, 1], r_m3[a][1])
        for half in range(2):
            vg4[a, pl.ds(half * 2, 2)] = (
                part[a, pl.ds(half * 2, 2), j].astype(F32)
                + m2[a, half].astype(F32)
                + m3[a, half].astype(F32)
            ).astype(BF)
        own = local(vg4.at[a, y], put)
        for r in range(1, NY):
            yy = (y + r) % NY
            send(vg4.at[a, yy], put, r_fin[a] + r, at_y(yy))
        return own

    def sum_old(a, oput):
        for t in range(NJ):
            arrived(rold.at[a, t], r_old[a] + t)
        og4[a] = (
            rold[a, 0].astype(F32) + rold[a, 1].astype(F32)
            + rold[a, 2].astype(F32) + rold[a, 3].astype(F32)
        ).astype(BF)
        oown_copy = local(og4.at[a, y], oput)
        for r in range(1, NY):
            yy = (y + r) % NY
            send(og4.at[a, yy], oput, r_ofin[a] + r, at_y(yy))
        return oown_copy

    def by_head(copy, base, whole):
        copy.wait()
        for r in range(1, NY):
            arrived(whole.at[:, col((y + NY - r) % NY)], base + r)

    loc_g.wait()
    first, second = pl.ds(0, 512), pl.ds(512, 512)
    for hp in range(2):
        rows_arrived(gb, r_g, hp)
        spread(hp)
    for c in range(5):
        vacc[c] = keys_grad(gl, c, first)
    for hp in range(2, 4):
        rows_arrived(gb, r_g, hp)
        spread(hp)
    for c in (1, 2, 3, 4, 0):
        keep(1, c, vacc[c] + keys_grad(gl, c, second))
        if c == 2:
            sum_low(1)
        if c == 4:
            sum_high(1)

    gather_end(1)
    r_dq = [take("r", 4) for _ in range(4)]

    def scores_grad(hp, i):
        gh = heads(gb, i, hp)
        inv = linv[i, :, lanes(hp)]
        slot = i % 2
        delta = None
        for c in range(i + 2):
            d = dot_nt(chunk(1, c), gh)
            sbuf[slot, c] = d
            add = jnp.sum(ebuf[UNIT[i, c], :, lanes(hp)].astype(F32) * d, axis=0, keepdims=True)
            delta = add if delta is None else delta + add
        delta = delta * inv
        acc = None
        for c in range(i + 2):
            t = (ebuf[UNIT[i, c], :, lanes(hp)].astype(F32) * (sbuf[slot, c] - delta)).astype(BF)
            ebuf[UNIT[i, c], :, lanes(hp)] = t
            term = dot(kt[c], t)
            acc = term if acc is None else acc + term
        acc = acc * (inv * SCALE)
        out = jnp.concatenate([acc[:, :HD].T, acc[:, HD:].T], axis=1)
        dqb[i, :, lanes(hp)] = out.astype(BF)

    loc_dq = []

    def send_dq(hp):
        at = pl.ds(hp * 256, 512)
        loc_dq.append(local(dqb.at[y, :, at], dq_ref.at[:, half_of(y, hp)]))
        for r in range(1, NY):
            yy = (y + r) % NY
            send(dqb.at[yy, :, at], dq_ref.at[:, half_of(y, hp)], r_dq[hp] + r, at_y(yy))

    for i in range(4):
        scores_grad(0, i)
    lax.fori_loop(0, 32, spread_q, 0, unroll=8)
    scores_grad(1, 0)
    scores_grad(1, 1)
    sum_merge(1)
    scores_grad(1, 2)
    scores_grad(1, 3)
    send_dq(0)
    scores_grad(2, 0)
    v_own = sum_end(1, vgall.at[dp, :, col(y)])
    for i in range(1, 4):
        scores_grad(2, i)
    r_vg = take("r", 4)
    r_vs = take("r", 4)
    by_head(v_own, r_fin[1], vgall.at[dp])
    sib = 2 * x + 1 - core
    for t in (1, 3, 2):
        send(vgall.at[dp], vgall.at[dp], r_vg + t, at_dp(2 * ((x + t) % 4) + core))
    send(vgall.at[dp], vgall.at[dp], r_vs, at_dp(sib))
    dv_copy = local(vgall.at[dp], dv_ref)
    for i in range(4):
        scores_grad(3, i)
    send_dq(2)
    for c in (1, 2):
        keep(0, c, keys_grad(ql, c))
    sum_low(0)
    for t in (1, 3, 2):
        d = 2 * ((x + 4 - t) % 4) + core
        arrived(vgall.at[d], r_vg + t)
        send(vgall.at[d], vgall.at[d], r_vs + t, at_dp(sib))

    loc_xx.wait()
    for t in range(1, NDP):
        arrived(xall.at[:, :, col((dp + NDP - t) % NDP)], r_x + t)
    for t in range(4):
        arrived(vgall.at[2 * ((x + 4 - t) % 4) + 1 - core], r_vs + t)
    r_wy = [take("r", 4), take("r", 4)]

    def weight(yy):
        left = xall[pl.ds(yy * 8, 8)].reshape(256, NDP * TOK)
        return dot(left, vgall[...].reshape(NDP * TOK, 4 * HD)).reshape(8, 32, 4 * HD)

    for r in (2, 1, 3):
        yy = (y + r) % NY
        both = weight(yy).astype(BF)
        wp[r - 1, 0] = both[:, :16]
        wp[r - 1, 1] = both[:, 16:]
        send(wp.at[r - 1, 0], ry.at[r - 1, 0], r_wy[0] + r, at_y(yy))
    for r in (2, 1, 3):
        send(wp.at[r - 1, 1], ry.at[r - 1, 1], r_wy[1] + r, at_y((y + r) % NY))
    for c in (3, 4):
        keep(0, c, keys_grad(ql, c))
    sum_high(0)
    keep(0, 0, keys_grad(ql, 0))
    ov_own = sum_old(1, odv_ref.at[:, col(y)])
    sum_merge(0)
    both = weight(y)
    wown[0] = both[:, :16]
    wown[1] = both[:, 16:]
    r_wz = [take("r", 8), take("r", 8)]
    r_wd = [take("r", 8), take("r", 8)]

    def weight_y(h):
        for r in range(1, NY):
            arrived(ry.at[r - 1, h], r_wy[h] + r)
        wz[h] = (
            wown[h] + ry[0, h].astype(F32) + ry[1, h].astype(F32) + ry[2, h].astype(F32)
        ).astype(BF)
        for t in (4, 3, 5, 2, 6, 1, 7):
            zz = (z + t) % 8
            send(wz.at[h, zz], rz.at[t - 1, h], r_wz[h] + t, at_j(zz // 2, zz % 2))

    def rows(d, h):
        return pl.ds(pl.multiple_of(d * 32 + h * 16, 16), 16)

    def weight_z(h):
        acc = wz[h, z].astype(F32)
        for t in range(1, 8):
            arrived(rz.at[t - 1, h], r_wz[h] + t)
            acc = acc + rz[t - 1, h].astype(F32)
        wfin[h] = (acc * (1.0 / 256.0)).astype(BF)
        own = local(wfin.at[h], dw_ref.at[rows(dp, h)])
        for t in (4, 3, 5, 2, 6, 1, 7):
            send(wfin.at[h], dw_ref.at[rows(dp, h)], r_wd[h] + t, at_dp((dp + t) % NDP))
        return own

    early = len(sends)
    weight_y(0)
    k_own = sum_end(0, dk_ref.at[:, col(y)])
    weight_y(1)
    ok_own = sum_old(0, odk_ref.at[:, col(y)])
    by_head(ov_own, r_ofin[1], odv_ref)
    dv_copy.wait()
    for hp in (0, 2):
        loc_dq[hp // 2].wait()
        for r in range(1, NY):
            arrived(dq_ref.at[:, half_of((y + NY - r) % NY, hp)], r_dq[hp] + r)
    for c in sends[:early]:
        c.wait_send()
    own_w = [weight_z(0), weight_z(1)]

    by_head(k_own, r_fin[0], dk_ref)
    by_head(ok_own, r_ofin[0], odk_ref)
    for h in range(2):
        own_w[h].wait()
        for t in range(1, NDP):
            arrived(dw_ref.at[rows((dp + NDP - t) % NDP, h)], r_wd[h] + t)
    for c in sends[early:]:
        c.wait_send()
    assert count["s"] <= ssem.shape[0] and count["r"] <= rsem.shape[0]
    assert count["l"] <= lsem.shape[0]


def deliver(*refs):
    source, target, held = refs[:6], refs[6:12], refs[12:18]
    sem_in, sem_out = refs[18:]
    inward = [pltpu.make_async_copy(source[n], held[n], sem_in.at[n]) for n in range(6)]
    outward = [pltpu.make_async_copy(held[n], target[n], sem_out.at[n]) for n in range(6)]
    for c in inward:
        c.start()
    for n in range(6):
        inward[n].wait()
        outward[n].start()
    for c in outward:
        c.wait()


def on_device(queries, keys, values, old_keys, old_values, out_grad, inputs, reads):
    anywhere = pl.BlockSpec(memory_space=pl.ANY)
    out = [(TOK, 4096), (TOK, 512), (TOK, 512), (OLDT, 512), (OLDT, 512), (256, 512)]
    bf = lambda *shape: pltpu.VMEM(shape, BF)
    f32 = lambda *shape: pltpu.VMEM(shape, F32)
    results = pl.pallas_call(
        kernel,
        out_shape=[jax.ShapeDtypeStruct(shape, BF) for shape in out],
        in_specs=[anywhere] * 7 + [pl.BlockSpec(memory_space=pltpu.SMEM)],
        out_specs=[anywhere] * 6,
        scratch_shapes=[
            bf(TOK, 8192),
            bf(32, 8, 32, TOK),
            bf(32, 32, NDP * TOK),
            bf(4, TOK, ROWS),
            bf(4, TOK, ROWS),
            bf(2, NY, NJ, TOK, HD),
            bf(2, NY, NJ, OLDT, HD),
            bf(2, NY, OLDT, HD),
            bf(5, HD, CHUNK),
            bf(len(UNITS), CHUNK, ROWS),
            f32(2, 5, CHUNK, 256),
            f32(4, 1, ROWS),
            f32(4, ROWS, HD),
            bf(4, ROWS, HD),
            bf(4, ROWS, HD),
            bf(4, TOK, ROWS),
            f32(5, CHUNK, HD),
            bf(2, NY, NJ, TOK, HD),
            bf(2, NY, NJ, OLDT, HD),
            bf(2, 2, 2, TOK, HD),
            bf(2, 2, 2, TOK, HD),
            bf(2, 2, 2, TOK, HD),
            bf(2, 2, 2, TOK, HD),
            bf(2, NJ, NY, OLDT, HD),
            bf(2, NY, TOK, HD),
            bf(2, NY, OLDT, HD),
            bf(NDP, TOK, 512),
            bf(3, 2, 8, 16, 512),
            f32(2, 8, 16, 512),
            bf(3, 2, 8, 16, 512),
            bf(2, 8, 16, 512),
            bf(7, 2, 16, 512),
            bf(2, 16, 512),
            pltpu.SemaphoreType.DMA((SENDS,)),
            pltpu.SemaphoreType.DMA((RECVS,)),
            pltpu.SemaphoreType.DMA((24,)),
        ],
        compiler_params=pltpu.CompilerParams(
            collective_id=0, has_side_effects=True, vmem_limit_bytes=56 * 1024 * 1024
        ),
        cost_estimate=pl.CostEstimate(
            flops=11_000_000_000, bytes_accessed=10_000_000, transcendentals=8_000_000
        ),
    )(
        queries[0, 0], keys[0, 0], values[0, 0], old_keys[0, 0], old_values[0, 0],
        out_grad[0, 0], inputs[0, 0], reads[0, 0],
    )
    results = pl.pallas_call(
        deliver,
        out_shape=[jax.ShapeDtypeStruct(shape, BF) for shape in out],
        in_specs=[anywhere] * 6,
        out_specs=[anywhere] * 6,
        scratch_shapes=[bf(*shape) for shape in out]
        + [pltpu.SemaphoreType.DMA((6,)), pltpu.SemaphoreType.DMA((6,))],
    )(*results)
    return tuple(r[None, None] for r in results[:5]) + (results[5],)


def solution(mesh):
    token = P("dp", "pool", "seq", None)
    in_specs = (token,) * 7 + (P("dp", "pool", None, None),)
    out_specs = (token,) * 5 + (P(("seq", "pool"), None),)
    return jax.shard_map(
        on_device, mesh=mesh, in_specs=in_specs, out_specs=out_specs, check_vma=False
    )
```
